128 devices in a mesh: aux: 4 (over z), pair: 32 (over x, y, core).
Axes of the slice: x: 4, y: 4, z: 4, core: 2. Of those that a mesh axis runs over, the one named last changes fastest.
Arguments:
- integrals: bfloat16 [96, 64, 1536, 128], P('pair', None, 'aux'), may hold values from -0.375 to 0.375
- coefficients: bfloat16 [8192, 64], P('pair'), may hold values from -6 to 6
- nu_blocks: int32 [4, 96], P('aux', 'pair'), may hold values from 0 to 63
- tile_count: int32 [4, 32], P('aux', 'pair'), may hold values from 1 to 3, as said below
- metric_root: bfloat16 [1536, 1536], replicated
Outputs:
- fitted: bfloat16 [64, 64, 32, 1536], P('aux', None, 'pair')
The draws below stay inside these ranges and needn't reach their ends.
Inputs may be any that keep to these rules, and one draw needn't show every extreme that they name: `nu_blocks`: a slot's basis row block covers basis functions 128 * v to 128 * v + 127; slots may repeat a block. `tile_count`: some device holds 3 live tiles in every draw.
All inputs are finite; a program needn't handle non-finite values.
Results may differ from the reference program's by a relative error of at most 0.005.
Values may be sent and summed in bfloat16 or wider, within the bound.
No kernel may reach another device: no remote copies, remote signals or barrier semaphores. Data moves between devices by JAX's collectives and lax.ppermute only.
A program may use at most 128 MiB of HBM per device.

```python
import math
import jax
import jax.numpy as jnp
from jax import lax

NAUX = 1536
NOCC = 64
NBF = 8192
NB = 128
KSLOT = 3
MU_DEV = 64
TILES = 96
NRB = 64
N_AUX = 4
N_PAIR = 32


def draw_tile_count(key, part):
    counts = jax.random.randint(key, (N_AUX, N_PAIR), 1, KSLOT + 1)
    chosen = jax.random.randint(jax.random.fold_in(key, 7), (), 0, N_AUX * N_PAIR)
    flat_index = jnp.arange(N_AUX * N_PAIR, dtype=jnp.int32).reshape(N_AUX, N_PAIR)
    return jnp.where(flat_index == chosen, KSLOT, counts).astype(jnp.int32)


def draw_metric_root(key, part):
    noise = jax.random.normal(key, (NAUX, NAUX), jnp.float32)
    diag_values = jax.random.uniform(jax.random.fold_in(key, 3), (NAUX,), jnp.float32, 1.0, 2.0)
    symmetric = (noise + noise.T) * 0.5 * (0.6 / math.sqrt(NAUX))
    positions = jnp.arange(NAUX, dtype=jnp.int32)
    on_diagonal = positions[:, None] == positions[None, :]
    return jnp.where(on_diagonal, diag_values[:, None] * jnp.ones((1, NAUX), jnp.float32), symmetric).astype(jnp.bfloat16)


def plant(drawn, own_key, least, top_value):
    place = [jax.random.randint(jax.random.fold_in(own_key, axis), (), 0, length) for axis, length in enumerate(drawn.shape)]
    widest = drawn.shape.index(max(drawn.shape))
    neighbour = place[:widest] + [(place[widest] + 1) % drawn.shape[widest]] + place[widest + 1:]
    return drawn.at[tuple(place)].set(least).at[tuple(neighbour)].set(top_value)


def level_of(rng, shape, cuts, smallest, high):
    def one(position, parts):
        steps = jax.random.uniform(jax.random.fold_in(jax.random.fold_in(rng, 6), position), (parts,), jnp.float32, smallest / len(cuts), high / len(cuts))
        return jnp.repeat(jnp.exp(steps), shape[position] // parts).reshape((-1,) + (1,) * (len(shape) - position - 1))

    level = one(*cuts[0])
    for cut in cuts[1:]:
        level = level * one(*cut)
    return level


def scatter_about(own_key, shape, width, limit, pieces=(), held_as=jnp.bfloat16):
    entries = jax.random.normal(own_key, shape, jnp.float32) * width
    if len(pieces) > 0:
        entries = level_of(own_key, shape, pieces, -0.22, 0.18) * entries
    return jnp.clip(entries, min=-limit, max=limit).astype(held_as)


def setup_inputs(seed: int = 0) -> dict:
    splits = jax.random.split(jax.random.key(seed), 6)
    integrals = scatter_about(splits[0], (TILES, MU_DEV, NAUX, NB), (2 * NB) ** -0.5, 0.375, ((0, 32), (2, 4)))
    coefficients = scatter_about(splits[1], (NBF, NOCC), 1.0, 6.0, ((0, 32),))
    nu_blocks = plant(jax.random.randint(splits[2], (N_AUX, TILES), 0, NRB), jax.random.fold_in(splits[2], 1), 0, NRB - 1).astype(jnp.int32)
    tile_count = draw_tile_count(jax.random.fold_in(splits[5], 71), 0)
    metric_root = draw_metric_root(jax.random.fold_in(splits[5], 71), 0)
    return dict(integrals=integrals, coefficients=coefficients, nu_blocks=nu_blocks, tile_count=tile_count, metric_root=metric_root)


def reference(integrals, coefficients, nu_blocks, tile_count, metric_root):
    aux_width = NAUX // N_AUX
    row_blocks = coefficients.reshape(NRB, NB, NOCC)
    picked = row_blocks[nu_blocks]
    picked = picked.reshape(N_AUX, N_PAIR, KSLOT, NB, NOCC).transpose(1, 2, 0, 3, 4)
    slot_ids = jnp.arange(TILES, dtype=jnp.int32) % KSLOT
    owner_ids = jnp.arange(TILES, dtype=jnp.int32) // KSLOT
    live = (slot_ids[None, :] < tile_count[:, owner_ids]).astype(jnp.float32)
    live = live.reshape(N_AUX, N_PAIR, KSLOT).transpose(1, 2, 0)
    tiles_home = integrals.reshape(N_PAIR, KSLOT, MU_DEV, NAUX, NB)

    def home_block(packed):
        tile_set, coeff_set, mask_set = packed
        running = jnp.zeros((NOCC, MU_DEV, N_AUX, aux_width), jnp.float32)
        for slot_index in range(KSLOT):
            split_tile = tile_set[slot_index].reshape(MU_DEV, N_AUX, aux_width, NB).astype(jnp.float32)
            term = jnp.einsum("manb,abi->iman", split_tile, coeff_set[slot_index].astype(jnp.float32))
            running = running + term * mask_set[slot_index][None, None, :, None]
        return running.reshape(NOCC, MU_DEV, NAUX).astype(jnp.bfloat16)

    half = lax.map(home_block, (tiles_home, picked, live))

    def fit_block(half_home):
        product = jnp.dot(half_home.reshape(NOCC * MU_DEV, NAUX), metric_root.T, preferred_element_type=jnp.float32)
        return product.astype(jnp.bfloat16).reshape(NOCC, MU_DEV, NAUX)

    fitted_home = lax.map(fit_block, half)
    return fitted_home.transpose(1, 2, 0, 3)
```

```python
import functools

import jax
import jax.numpy as jnp
from jax import lax
from jax.experimental import pallas as pl
from jax.experimental.pallas import tpu as pltpu
from jax.sharding import PartitionSpec as P

NT = (((1,), (1,)), ((), ()))
VMEM = pl.BlockSpec(memory_space=pltpu.VMEM)
SMEM = pl.BlockSpec(memory_space=pltpu.SMEM)
HBM = pl.BlockSpec(memory_space=pltpu.HBM)

SIDE = 4
GROUP = 16
BLOCK = 4
CHUNKS = ((0, 16), (32, 32), (16, 16))
OFFSETS = (0, 2, 1, 3)


def place_of(offset):
    return jnp.where(offset == 2, 1, jnp.where(offset == 1, 2, offset))


def coords(p):
    return p // (2 * SIDE), (p // 2) % SIDE, p % 2


def line_perm(phase, step):
    pairs = []
    for p in range(2 * SIDE * SIDE):
        x, y, core = coords(p)
        if core == phase:
            x = (x + step) % SIDE
        else:
            y = (y + step) % SIDE
        pairs.append((p, (x * SIDE + y) * 2 + core))
    return pairs


def gather_coeff(coeff_t):
    mine = coeff_t[None]
    for phase in (0, 1):
        mine = jnp.concatenate(
            [mine] + [lax.ppermute(mine, "pair", line_perm(phase, step)) for step in OFFSETS[1:]], 0
        )
    partner = lax.ppermute(mine, "pair", [(p, p ^ 1) for p in range(2 * SIDE * SIDE)])
    return mine, partner


def pick_coeff(nu_ref, count_ref, mine_ref, partner_ref, cc_ref):
    aux = lax.axis_index("aux")
    pair = lax.axis_index("pair")
    my_x, my_y, my_core = coords(pair)
    width = cc_ref.shape[1] // 3
    for slot in range(3):
        block = nu_ref[0, slot]
        x, y, core = coords(block // 2)
        step_x = place_of((my_x - x + SIDE) % SIDE)
        step_y = place_of((my_y - y + SIDE) % SIDE)
        piece = jnp.where(core == 0, step_y * SIDE + step_x, step_x * SIDE + step_y)
        lanes = pl.ds(pl.multiple_of((block % 2) * width, width), width)
        live = slot < count_ref[0, 0]
        for d in range(SIDE):
            rows = pl.ds(pl.multiple_of(((aux + d) % SIDE) * 16, 16), 16)
            own = mine_ref[piece, rows, lanes]
            other = partner_ref[piece, rows, lanes]
            chosen = jnp.where(core == my_core, own, other)
            cc_ref[16 * d:16 * d + 16, width * slot:width * (slot + 1)] = jnp.where(
                live, chosen, jnp.zeros_like(chosen)
            )


def half_body(first, count, integrals_ref, cc_ref, out_refs, tiles, acc, sems, before_dots):
    copies = []
    for b in range(count // BLOCK):
        copy = pltpu.make_async_copy(
            integrals_ref.at[:, pl.ds(first + b * BLOCK, BLOCK)], tiles.at[b], sems.at[b]
        )
        copy.start()
        copies.append(copy)
    before_dots()
    cc = cc_ref[...]
    width = tiles.shape[3]
    parts = width // 128
    for g in range(count // GROUP):
        for k in range(GROUP // BLOCK):
            b = g * (GROUP // BLOCK) + k
            copies[b].wait()
            tile = jnp.concatenate([tiles[b, s].reshape(BLOCK * width, 128) for s in range(3)], axis=1)
            prod = lax.dot_general(cc, tile, NT, preferred_element_type=jnp.float32)
            for j in range(BLOCK):
                for q in range(parts):
                    lane = (j * parts + q) * 128
                    acc[g, q, pl.ds(k * BLOCK + j, 64, stride=GROUP), :] = prod[:, lane:lane + 128]
        for d in range(SIDE):
            for q in range(parts):
                rows = acc[g, q, 256 * d:256 * d + 256, :].astype(jnp.bfloat16)
                out_refs[d][:, GROUP * g:GROUP * (g + 1), 128 * q:128 * (q + 1)] = rows.reshape(16, GROUP, 128)


def half_first(first, count, nu_ref, count_ref, mine_ref, partner_ref, integrals_ref,
               o0, o1, o2, o3, cc_ref, tiles, acc, sems):
    def before():
        pick_coeff(nu_ref, count_ref, mine_ref, partner_ref, cc_ref)

    half_body(first, count, integrals_ref, cc_ref, (o0, o1, o2, o3), tiles, acc, sems, before)


def half_next(first, count, cc_ref, integrals_ref, o0, o1, o2, o3, tiles, acc, sems):
    half_body(first, count, integrals_ref, cc_ref, (o0, o1, o2, o3), tiles, acc, sems, lambda: None)


def half_call(first, count, integrals, cc=None, picked_from=None):
    width = integrals.shape[2]
    outs = [jax.ShapeDtypeStruct((16, count, width), jnp.bfloat16)] * SIDE
    common = dict(
        scratch_shapes=[
            pltpu.VMEM((count // BLOCK, 3, BLOCK, width, 128), jnp.bfloat16),
            pltpu.VMEM((count // GROUP, width // 128, 64 * GROUP, 128), jnp.float32),
            pltpu.SemaphoreType.DMA((count // BLOCK,)),
        ],
        compiler_params=pltpu.CompilerParams(vmem_limit_bytes=48 * 2**20),
        cost_estimate=pl.CostEstimate(
            flops=2 * count * width * 384 * 256, bytes_accessed=count * width * 384 * 2, transcendentals=0
        ),
    )
    if cc is None:
        res = pl.pallas_call(
            functools.partial(half_first, first, count),
            in_specs=[SMEM, SMEM, VMEM, VMEM, HBM],
            out_specs=[VMEM] * 5,
            out_shape=outs + [jax.ShapeDtypeStruct((64, 384), jnp.bfloat16)],
            **common,
        )(*picked_from, integrals)
        return res[:SIDE], res[SIDE]
    res = pl.pallas_call(
        functools.partial(half_next, first, count),
        in_specs=[VMEM, HBM],
        out_specs=[VMEM] * 4,
        out_shape=outs,
        **common,
    )(cc, integrals)
    return res, cc


def fit_kernel(first, count, *refs):
    a_refs, root_ref, (out_ref, stage, sems) = refs[:4], refs[4], refs[-3:]
    rows = 16 * count
    step = stage.shape[3]
    arrived = jnp.concatenate([a[...].reshape(rows, a.shape[2]) for a in a_refs], axis=1)
    copies = []
    for q in range(stage.shape[0]):
        prod = lax.dot_general(
            arrived, root_ref[q * step:(q + 1) * step, :], NT, preferred_element_type=jnp.float32
        )
        stage[q] = prod.astype(jnp.bfloat16).reshape(16, count, step)
        copy = pltpu.make_async_copy(
            stage.at[q], out_ref.at[:, pl.ds(first, count), pl.ds(q * step, step)], sems.at[q]
        )
        copy.start()
        copies.append(copy)
    for copy in copies:
        copy.wait()


def fit_call(first, count, arrived, root, out):
    total = root.shape[0]
    step = 512
    operands = list(arrived) + [root]
    specs = [VMEM] * 5
    aliases = {}
    if out is not None:
        operands.append(out)
        specs.append(HBM)
        aliases = {5: 0}
    return pl.pallas_call(
        functools.partial(fit_kernel, first, count),
        in_specs=specs,
        out_specs=HBM,
        out_shape=jax.ShapeDtypeStruct((16, 64, total), jnp.bfloat16),
        scratch_shapes=[
            pltpu.VMEM((total // step, 16, count, step), jnp.bfloat16),
            pltpu.SemaphoreType.DMA((total // step,)),
        ],
        input_output_aliases=aliases,
        compiler_params=pltpu.CompilerParams(vmem_limit_bytes=24 * 2**20),
        cost_estimate=pl.CostEstimate(
            flops=2 * 16 * count * total * total, bytes_accessed=16 * count * total * 4, transcendentals=0
        ),
    )(*operands)


def shards(integrals, coefficients, nu_blocks, tile_count, metric_root):
    aux = lax.axis_index("aux")
    width = integrals.shape[2]
    root = jnp.concatenate(
        [
            lax.dynamic_slice_in_dim(metric_root, ((aux - d + SIDE) % SIDE) * width, width, 1)
            for d in range(SIDE)
        ],
        axis=1,
    )
    mine, partner = gather_coeff(coefficients.T)
    cc = None
    held = []
    for first, count in CHUNKS:
        parts, cc = half_call(first, count, integrals, cc, (nu_blocks, tile_count, mine, partner))
        sent = {
            d: lax.ppermute(parts[d], "aux", [(i, (i + d) % SIDE) for i in range(SIDE)]) for d in (2, 1, 3)
        }
        held.append((parts[0], sent[1], sent[2], sent[3]))
    out = None
    for (first, count), arrived in zip(CHUNKS, held):
        out = fit_call(first, count, arrived, root, out)
    return out.reshape(out.shape[0], out.shape[1], 1, out.shape[2])


def solution(mesh):
    placed = (
        P("pair", None, "aux", None),
        P("pair", None),
        P("aux", "pair"),
        P("aux", "pair"),
        P(),
    )
    return jax.shard_map(
        shards, mesh=mesh, in_specs=placed, out_specs=P("aux", None, "pair", None), check_vma=False
    )
```

```python
import functools

import jax
import jax.numpy as jnp
from jax import lax
from jax.experimental import pallas as pl
from jax.experimental.pallas import tpu as pltpu
from jax.sharding import PartitionSpec as P

NT = (((1,), (1,)), ((), ()))
VMEM = pl.BlockSpec(memory_space=pltpu.VMEM)
SMEM = pl.BlockSpec(memory_space=pltpu.SMEM)
HBM = pl.BlockSpec(memory_space=pltpu.HBM)

SIDE = 4
GROUP = 16
BLOCK = 4
CHUNKS = ((0, 16), (16, 32), (48, 16))
STAGED = 24
HOPS = (0, 1, 2, 3)
LINES = ((0, 2, 1, 3), (0, 3, 1, 2))


def place_of(phase, step):
    place = 0
    for k, other in enumerate(LINES[phase]):
        place = jnp.where(step == other, k, place)
    return place


def coords(p):
    return p // (2 * SIDE), (p // 2) % SIDE, p % 2


def line_perm(phase, step):
    pairs = []
    for p in range(2 * SIDE * SIDE):
        x, y, core = coords(p)
        if core == phase:
            x = (x + step) % SIDE
        else:
            y = (y + step) % SIDE
        pairs.append((p, (x * SIDE + y) * 2 + core))
    return pairs


def gather_coeff(coeff_t, integrals):
    own = coeff_t[None]
    tiles = stage_call(integrals)
    line = jnp.concatenate(
        [own] + [lax.ppermute(own, "pair", line_perm(0, step)) for step in LINES[0][1:]], 0
    )
    line, tiles = lax.optimization_barrier((line, tiles))
    mine = [line] + [lax.ppermute(line, "pair", line_perm(1, step)) for step in LINES[1][1:]]
    swap = [(p, p ^ 1) for p in range(2 * SIDE * SIDE)]
    partner = [lax.ppermute(lines, "pair", swap) for lines in mine]
    return mine + partner, tiles


def pick_coeff(nu_ref, count_ref, coeff_refs, cc_ref):
    aux = lax.axis_index("aux")
    pair = lax.axis_index("pair")
    my_x, my_y, my_core = coords(pair)
    width = cc_ref.shape[1] // 3
    for slot in range(3):
        block = nu_ref[0, slot]
        x, y, core = coords(block // 2)
        step_x = (my_x - x + SIDE) % SIDE
        step_y = (my_y - y + SIDE) % SIDE
        first_step = place_of(0, jnp.where(core == 0, step_x, step_y))
        second_step = place_of(1, jnp.where(core == 0, step_y, step_x))
        which = jnp.where(core == my_core, 0, SIDE) + second_step
        lanes = pl.ds(pl.multiple_of((block % 2) * width, width), width)
        live = slot < count_ref[0, 0]
        for d in range(SIDE):
            rows = pl.ds(pl.multiple_of(((aux + d) % SIDE) * 16, 16), 16)
            chosen = coeff_refs[0][first_step, rows, lanes]
            for k in range(1, 2 * SIDE):
                chosen = jnp.where(which == k, coeff_refs[k][first_step, rows, lanes], chosen)
            cc_ref[16 * d:16 * d + 16, width * slot:width * (slot + 1)] = jnp.where(
                live, chosen, jnp.zeros_like(chosen)
            )


def stage_kernel(integrals_ref, tiles_ref, sems):
    copies = []
    for b in range(STAGED // BLOCK):
        copy = pltpu.make_async_copy(integrals_ref.at[:, pl.ds(b * BLOCK, BLOCK)], tiles_ref.at[b], sems.at[b])
        copy.start()
        copies.append(copy)
    for copy in copies:
        copy.wait()


def stage_call(integrals):
    return pl.pallas_call(
        stage_kernel,
        in_specs=[HBM],
        out_specs=VMEM,
        out_shape=jax.ShapeDtypeStruct((STAGED // BLOCK, 3, BLOCK) + integrals.shape[2:], integrals.dtype),
        scratch_shapes=[pltpu.SemaphoreType.DMA((STAGED // BLOCK,))],
        compiler_params=pltpu.CompilerParams(vmem_limit_bytes=40 * 2**20),
        cost_estimate=pl.CostEstimate(
            flops=0, bytes_accessed=2 * STAGED * integrals.shape[2] * 384 * 2, transcendentals=0
        ),
    )(integrals)


def half_body(count, cc_ref, out_refs, acc, block):
    cc = cc_ref[...]
    width = out_refs[0].shape[2]
    parts = width // 128
    for g in range(count // GROUP):
        for k in range(GROUP // BLOCK):
            b = g * (GROUP // BLOCK) + k
            tiles, at = block(b)
            tile = jnp.concatenate([tiles[at, s].reshape(BLOCK * width, 128) for s in range(3)], axis=1)
            prod = lax.dot_general(cc, tile, NT, preferred_element_type=jnp.float32)
            for j in range(BLOCK):
                for q in range(parts):
                    lane = (j * parts + q) * 128
                    acc[g, q, pl.ds(k * BLOCK + j, 64, stride=GROUP), :] = prod[:, lane:lane + 128]
        for d in range(SIDE):
            for q in range(parts):
                rows = acc[g, q, 256 * d:256 * d + 256, :].astype(jnp.bfloat16)
                out_refs[d][:, GROUP * g:GROUP * (g + 1), 128 * q:128 * (q + 1)] = rows.reshape(16, GROUP, 128)


def half_first(count, nu_ref, count_ref, *refs):
    coeff_refs, (tiles, o0, o1, o2, o3, cc_ref, acc) = refs[:2 * SIDE], refs[2 * SIDE:]
    pick_coeff(nu_ref, count_ref, coeff_refs, cc_ref)
    half_body(count, cc_ref, (o0, o1, o2, o3), acc, lambda b: (tiles, b))


def half_next(first, count, held, cc_ref, integrals_ref, *refs):
    o0, o1, o2, o3, acc, tiles, sems = refs[-7:]
    copies = []
    for b in range(held, count // BLOCK):
        copy = pltpu.make_async_copy(
            integrals_ref.at[:, pl.ds(first + b * BLOCK, BLOCK)], tiles.at[b - held], sems.at[b - held]
        )
        copy.start()
        copies.append(copy)

    def block(b):
        if b < held:
            return refs[0], CHUNKS[0][1] // BLOCK + b
        copies[b - held].wait()
        return tiles, b - held

    half_body(count, cc_ref, (o0, o1, o2, o3), acc, block)


def half_call(first, count, integrals, tiles, cc, picked_from):
    width = integrals.shape[2]
    outs = [jax.ShapeDtypeStruct((16, count, width), jnp.bfloat16)] * SIDE
    acc = pltpu.VMEM((count // GROUP, width // 128, 64 * GROUP, 128), jnp.float32)
    cost = pl.CostEstimate(
        flops=2 * count * width * 384 * 256, bytes_accessed=count * width * 384 * 2, transcendentals=0
    )
    if cc is None:
        res = pl.pallas_call(
            functools.partial(half_first, count),
            in_specs=[SMEM, SMEM] + [VMEM] * (2 * SIDE + 1),
            out_specs=[VMEM] * 5,
            out_shape=outs + [jax.ShapeDtypeStruct((64, 384), jnp.bfloat16)],
            scratch_shapes=[acc],
            compiler_params=pltpu.CompilerParams(vmem_limit_bytes=24 * 2**20),
            cost_estimate=cost,
        )(*picked_from, tiles)
        return res[:SIDE], res[SIDE]
    operands, specs, held = [cc, integrals], [VMEM, HBM], 0
    if first < STAGED:
        operands.append(tiles)
        specs.append(VMEM)
        held = (STAGED - first) // BLOCK
    copied = count // BLOCK - held
    res = pl.pallas_call(
        functools.partial(half_next, first, count, held),
        in_specs=specs,
        out_specs=[VMEM] * 4,
        out_shape=outs,
        scratch_shapes=[
            acc,
            pltpu.VMEM((copied, 3, BLOCK, width, 128), jnp.bfloat16),
            pltpu.SemaphoreType.DMA((copied,)),
        ],
        compiler_params=pltpu.CompilerParams(vmem_limit_bytes=42 * 2**20),
        cost_estimate=cost,
    )(*operands)
    return res, cc


def arrange_kernel(root_ref, after_ref, out_ref, sems):
    aux = lax.axis_index("aux")
    width = out_ref.shape[1] // SIDE
    copies = []
    for k, d in enumerate(HOPS):
        source = pl.ds(pl.multiple_of(((aux - d + SIDE) % SIDE) * width, 128), width)
        copy = pltpu.make_async_copy(
            root_ref.at[:, source], out_ref.at[:, pl.ds(k * width, width)], sems.at[k]
        )
        copy.start()
        copies.append(copy)
    for copy in copies:
        copy.wait()


def arrange_root(root, after):
    return pl.pallas_call(
        arrange_kernel,
        in_specs=[HBM, HBM],
        out_specs=VMEM,
        out_shape=jax.ShapeDtypeStruct(root.shape, root.dtype),
        scratch_shapes=[pltpu.SemaphoreType.DMA((SIDE,))],
        compiler_params=pltpu.CompilerParams(vmem_limit_bytes=40 * 2**20),
        cost_estimate=pl.CostEstimate(flops=0, bytes_accessed=root.size // 64, transcendentals=0),
    )(root, after)


def fit_kernel(first, count, *refs):
    a_refs, root_ref, (out_ref, stage, sems) = refs[:4], refs[4], refs[-3:]
    rows = 16 * count
    step = stage.shape[3]
    arrived = jnp.concatenate([a[...].reshape(rows, a.shape[2]) for a in a_refs], axis=1)
    copies = []
    for q in range(stage.shape[0]):
        prod = lax.dot_general(
            arrived, root_ref[q * step:(q + 1) * step, :], NT, preferred_element_type=jnp.float32
        )
        stage[q] = prod.astype(jnp.bfloat16).reshape(16, count, step)
        copy = pltpu.make_async_copy(
            stage.at[q], out_ref.at[:, pl.ds(first, count), pl.ds(q * step, step)], sems.at[q]
        )
        copy.start()
        copies.append(copy)
    for copy in copies:
        copy.wait()


def fit_call(first, count, arrived, root, out):
    total = root.shape[0]
    step = total if count == GROUP else 512
    operands = list(arrived) + [root]
    specs = [VMEM] * 5
    aliases = {}
    if out is not None:
        operands.append(out)
        specs.append(HBM)
        aliases = {5: 0}
    return pl.pallas_call(
        functools.partial(fit_kernel, first, count),
        in_specs=specs,
        out_specs=HBM,
        out_shape=jax.ShapeDtypeStruct((16, 64, total), jnp.bfloat16),
        scratch_shapes=[
            pltpu.VMEM((total // step, 16, count, step), jnp.bfloat16),
            pltpu.SemaphoreType.DMA((total // step,)),
        ],
        input_output_aliases=aliases,
        compiler_params=pltpu.CompilerParams(vmem_limit_bytes=24 * 2**20),
        cost_estimate=pl.CostEstimate(
            flops=32 * count * total * total, bytes_accessed=16 * count * total * 4, transcendentals=0
        ),
    )(*operands)


def shards(integrals, coefficients, nu_blocks, tile_count, metric_root):
    coeff, tiles = gather_coeff(coefficients.T, integrals)
    cc = None
    held = []
    for k, (first, count) in enumerate(CHUNKS):
        if k >= 2:
            cc, held[k - 2] = lax.optimization_barrier((cc, held[k - 2]))
        parts, cc = half_call(first, count, integrals, tiles, cc, [nu_blocks, tile_count] + coeff)
        held.append(
            [parts[0]]
            + [lax.ppermute(parts[d], "aux", [(i, (i + d) % SIDE) for i in range(SIDE)]) for d in HOPS[1:]]
        )
    root = arrange_root(metric_root, parts[0])
    out = None
    for (first, count), arrived in zip(CHUNKS, held):
        out = fit_call(first, count, arrived, root, out)
    return out.reshape(out.shape[0], out.shape[1], 1, out.shape[2])


def solution(mesh):
    placed = (
        P("pair", None, "aux", None),
        P("pair", None),
        P("aux", "pair"),
        P("aux", "pair"),
        P(),
    )
    return jax.shard_map(
        shards, mesh=mesh, in_specs=placed, out_specs=P("aux", None, "pair", None), check_vma=False
    )
```

```python
import functools

import jax
import jax.numpy as jnp
from jax import lax
from jax.experimental import pallas as pl
from jax.experimental.pallas import tpu as pltpu
from jax.sharding import PartitionSpec as P

NT = (((1,), (1,)), ((), ()))
VMEM = pl.BlockSpec(memory_space=pltpu.VMEM)
SMEM = pl.BlockSpec(memory_space=pltpu.SMEM)
HBM = pl.BlockSpec(memory_space=pltpu.HBM)

SIDE = 4
GROUP = 16
BLOCK = 4
CHUNKS = ((0, 16), (16, 32), (48, 16))
SENDS = ((0, 1, 3, 2), (0, 3, 1, 2), (0, 1, 3, 2))
STAGED = 24
HOPS = (0, 1, 3, 2)
LINES = ((0, 2, 1, 3), (0, 3, 1, 2))


def place_of(phase, step):
    place = 0
    for k, other in enumerate(LINES[phase]):
        place = jnp.where(step == other, k, place)
    return place


def hop(k, core):
    return (HOPS[k] * (1 - 2 * core)) % SIDE


def coords(p):
    return p // (2 * SIDE), (p // 2) % SIDE, p % 2


def line_perm(phase, step):
    pairs = []
    for p in range(2 * SIDE * SIDE):
        x, y, core = coords(p)
        if core == phase:
            x = (x + step) % SIDE
        else:
            y = (y + step) % SIDE
        pairs.append((p, (x * SIDE + y) * 2 + core))
    return pairs


def aux_perm(k):
    pairs = 2 * SIDE * SIDE
    return [(a * pairs + p, (a + hop(k, p % 2)) % SIDE * pairs + p) for a in range(SIDE) for p in range(pairs)]


def gather_coeff(coeff_t, integrals):
    own = coeff_t[None]
    tiles = stage_call(integrals)
    line = jnp.concatenate(
        [own] + [lax.ppermute(own, "pair", line_perm(0, step)) for step in LINES[0][1:]], 0
    )
    line, tiles = lax.optimization_barrier((line, tiles))
    mine = [line] + [lax.ppermute(line, "pair", line_perm(1, step)) for step in LINES[1][1:]]
    swap = [(p, p ^ 1) for p in range(2 * SIDE * SIDE)]
    partner = [lax.ppermute(lines, "pair", swap) for lines in mine]
    return mine + partner, tiles


def pick_coeff(nu_ref, count_ref, coeff_refs, cc_ref):
    aux = lax.axis_index("aux")
    pair = lax.axis_index("pair")
    my_x, my_y, my_core = coords(pair)
    width = cc_ref.shape[1] // 3
    for slot in range(3):
        block = nu_ref[0, slot]
        x, y, core = coords(block // 2)
        step_x = (my_x - x + SIDE) % SIDE
        step_y = (my_y - y + SIDE) % SIDE
        first_step = place_of(0, jnp.where(core == 0, step_x, step_y))
        second_step = place_of(1, jnp.where(core == 0, step_y, step_x))
        which = jnp.where(core == my_core, 0, SIDE) + second_step
        lanes = pl.ds(pl.multiple_of((block % 2) * width, width), width)
        live = jnp.broadcast_to(count_ref[...], (16, width)) > slot
        for d in range(SIDE):
            step = jnp.where(my_core == 0, hop(d, 0), hop(d, 1))
            rows = pl.ds(pl.multiple_of(((aux + step) % SIDE) * 16, 16), 16)
            chosen = coeff_refs[0][first_step, rows, lanes]
            for k in range(1, 2 * SIDE):
                chosen = jnp.where(which == k, coeff_refs[k][first_step, rows, lanes], chosen)
            chosen = jnp.where(live, chosen.astype(jnp.float32), 0.0)
            cc_ref[16 * d:16 * d + 16, width * slot:width * (slot + 1)] = chosen.astype(jnp.bfloat16)


def stage_kernel(integrals_ref, tiles_ref, sems):
    copies = []
    for b in range(STAGED // BLOCK):
        copy = pltpu.make_async_copy(integrals_ref.at[:, pl.ds(b * BLOCK, BLOCK)], tiles_ref.at[b], sems.at[b])
        copy.start()
        copies.append(copy)
    for copy in copies:
        copy.wait()


def stage_call(integrals):
    return pl.pallas_call(
        stage_kernel,
        in_specs=[HBM],
        out_specs=VMEM,
        out_shape=jax.ShapeDtypeStruct((STAGED // BLOCK, 3, BLOCK) + integrals.shape[2:], integrals.dtype),
        scratch_shapes=[pltpu.SemaphoreType.DMA((STAGED // BLOCK,))],
        compiler_params=pltpu.CompilerParams(vmem_limit_bytes=40 * 2**20),
        cost_estimate=pl.CostEstimate(
            flops=0, bytes_accessed=2 * STAGED * integrals.shape[2] * 384 * 2, transcendentals=0
        ),
    )(integrals)


def half_body(count, cc_ref, out_refs, acc, block):
    cc = cc_ref[...]
    width = out_refs[0].shape[2]
    parts = width // 128
    for g in range(count // GROUP):
        for k in range(GROUP // BLOCK):
            b = g * (GROUP // BLOCK) + k
            tiles, at = block(b)
            tile = jnp.concatenate([tiles[at, s].reshape(BLOCK * width, 128) for s in range(3)], axis=1)
            prod = lax.dot_general(cc, tile, NT, preferred_element_type=jnp.float32)
            for j in range(BLOCK):
                for q in range(parts):
                    lane = (j * parts + q) * 128
                    acc[g, q, pl.ds(k * BLOCK + j, 64, stride=GROUP), :] = prod[:, lane:lane + 128]
        for d in range(SIDE):
            for q in range(parts):
                rows = acc[g, q, 256 * d:256 * d + 256, :].astype(jnp.bfloat16)
                out_refs[d][:, GROUP * g:GROUP * (g + 1), 128 * q:128 * (q + 1)] = rows.reshape(16, GROUP, 128)


def half_first(count, nu_ref, count_ref, *refs):
    coeff_refs, (tiles, o0, o1, o2, o3, cc_ref, acc) = refs[:2 * SIDE], refs[2 * SIDE:]
    pick_coeff(nu_ref, count_ref, coeff_refs, cc_ref)
    half_body(count, cc_ref, (o0, o1, o2, o3), acc, lambda b: (tiles, b))


def half_next(first, count, held, cc_ref, integrals_ref, *refs):
    o0, o1, o2, o3, acc, tiles, sems = refs[-7:]
    copies = []
    for b in range(held, count // BLOCK):
        copy = pltpu.make_async_copy(
            integrals_ref.at[:, pl.ds(first + b * BLOCK, BLOCK)], tiles.at[b - held], sems.at[b - held]
        )
        copy.start()
        copies.append(copy)

    def block(b):
        if b < held:
            return refs[0], CHUNKS[0][1] // BLOCK + b
        copies[b - held].wait()
        return tiles, b - held

    half_body(count, cc_ref, (o0, o1, o2, o3), acc, block)


def half_call(first, count, integrals, tiles, cc, picked_from):
    width = integrals.shape[2]
    outs = [jax.ShapeDtypeStruct((16, count, width), jnp.bfloat16)] * SIDE
    acc = pltpu.VMEM((count // GROUP, width // 128, 64 * GROUP, 128), jnp.float32)
    cost = pl.CostEstimate(
        flops=2 * count * width * 384 * 256, bytes_accessed=count * width * 384 * 2, transcendentals=0
    )
    if cc is None:
        res = pl.pallas_call(
            functools.partial(half_first, count),
            in_specs=[SMEM] + [VMEM] * (2 * SIDE + 2),
            out_specs=[VMEM] * 5,
            out_shape=outs + [jax.ShapeDtypeStruct((64, 384), jnp.bfloat16)],
            scratch_shapes=[acc],
            compiler_params=pltpu.CompilerParams(vmem_limit_bytes=24 * 2**20),
            cost_estimate=cost,
        )(*picked_from, tiles)
        return res[:SIDE], res[SIDE]
    operands, specs, held = [cc, integrals], [VMEM, HBM], 0
    if first < STAGED:
        operands.append(tiles)
        specs.append(VMEM)
        held = (STAGED - first) // BLOCK
    copied = count // BLOCK - held
    res = pl.pallas_call(
        functools.partial(half_next, first, count, held),
        in_specs=specs,
        out_specs=[VMEM] * 4,
        out_shape=outs,
        scratch_shapes=[
            acc,
            pltpu.VMEM((copied, 3, BLOCK, width, 128), jnp.bfloat16),
            pltpu.SemaphoreType.DMA((copied,)),
        ],
        compiler_params=pltpu.CompilerParams(vmem_limit_bytes=42 * 2**20),
        cost_estimate=cost,
    )(*operands)
    return res, cc


def arrange_kernel(root_ref, after_ref, out_ref, sems):
    aux = lax.axis_index("aux")
    core = lax.axis_index("pair") % 2
    width = out_ref.shape[1] // SIDE
    copies = []
    for k in range(SIDE):
        step = jnp.where(core == 0, hop(k, 0), hop(k, 1))
        source = pl.ds(pl.multiple_of(((aux - step + SIDE) % SIDE) * width, 128), width)
        copy = pltpu.make_async_copy(
            root_ref.at[:, source], out_ref.at[:, pl.ds(k * width, width)], sems.at[k]
        )
        copy.start()
        copies.append(copy)
    for copy in copies:
        copy.wait()


def arrange_root(root, after):
    return pl.pallas_call(
        arrange_kernel,
        in_specs=[HBM, HBM],
        out_specs=VMEM,
        out_shape=jax.ShapeDtypeStruct(root.shape, root.dtype),
        scratch_shapes=[pltpu.SemaphoreType.DMA((SIDE,))],
        compiler_params=pltpu.CompilerParams(vmem_limit_bytes=40 * 2**20),
        cost_estimate=pl.CostEstimate(flops=0, bytes_accessed=root.size // 64, transcendentals=0),
    )(root, after)


def fit_kernel(first, count, order, *refs):
    root_ref, (out_ref, stage, sems) = refs[4], refs[-3:]
    a_refs = [refs[order.index(k)] for k in range(SIDE)]
    rows = 16 * count
    step = stage.shape[3]
    arrived = jnp.concatenate([a[...].reshape(rows, a.shape[2]) for a in a_refs], axis=1)
    copies = []
    for q in range(stage.shape[0]):
        prod = lax.dot_general(
            arrived, root_ref[q * step:(q + 1) * step, :], NT, preferred_element_type=jnp.float32
        )
        stage[q] = prod.astype(jnp.bfloat16).reshape(16, count, step)
        copy = pltpu.make_async_copy(
            stage.at[q], out_ref.at[:, pl.ds(first, count), pl.ds(q * step, step)], sems.at[q]
        )
        copy.start()
        copies.append(copy)
    for copy in copies:
        copy.wait()


def fit_call(first, count, order, arrived, root, out):
    total = root.shape[0]
    step = total if count == GROUP else 512
    operands = [arrived[k] for k in order] + [root]
    specs = [VMEM] * 5
    aliases = {}
    if out is not None:
        operands.append(out)
        specs.append(HBM)
        aliases = {5: 0}
    return pl.pallas_call(
        functools.partial(fit_kernel, first, count, order),
        in_specs=specs,
        out_specs=HBM,
        out_shape=jax.ShapeDtypeStruct((16, 64, total), jnp.bfloat16),
        scratch_shapes=[
            pltpu.VMEM((total // step, 16, count, step), jnp.bfloat16),
            pltpu.SemaphoreType.DMA((total // step,)),
        ],
        input_output_aliases=aliases,
        compiler_params=pltpu.CompilerParams(vmem_limit_bytes=24 * 2**20),
        cost_estimate=pl.CostEstimate(
            flops=32 * count * total * total, bytes_accessed=16 * count * total * 4, transcendentals=0
        ),
    )(*operands)


def shards(integrals, coefficients, nu_blocks, tile_count, metric_root):
    coeff, tiles = gather_coeff(coefficients.T, integrals)
    cc = None
    held = []
    for k, (first, count) in enumerate(CHUNKS):
        if k >= 2:
            cc, held[k - 2] = lax.optimization_barrier((cc, held[k - 2]))
        parts, cc = half_call(first, count, integrals, tiles, cc, [nu_blocks, tile_count] + coeff)
        held.append(
            [parts[0]]
            + [lax.ppermute(parts[d], ("aux", "pair"), aux_perm(d)) for d in range(1, SIDE)]
        )
    root = arrange_root(metric_root, parts[0])
    out = None
    for (first, count), order, arrived in zip(CHUNKS, SENDS, held):
        out = fit_call(first, count, order, arrived, root, out)
    return out.reshape(out.shape[0], out.shape[1], 1, out.shape[2])


def solution(mesh):
    placed = (
        P("pair", None, "aux", None),
        P("pair", None),
        P("aux", "pair"),
        P("aux", "pair"),
        P(),
    )
    return jax.shard_map(
        shards, mesh=mesh, in_specs=placed, out_specs=P("aux", None, "pair", None), check_vma=False
    )
```

```python
import functools

import jax
import jax.numpy as jnp
from jax import lax
from jax.experimental import pallas as pl
from jax.experimental.pallas import tpu as pltpu
from jax.sharding import PartitionSpec as P

NT = (((1,), (1,)), ((), ()))
VMEM = pl.BlockSpec(memory_space=pltpu.VMEM)
SMEM = pl.BlockSpec(memory_space=pltpu.SMEM)
HBM = pl.BlockSpec(memory_space=pltpu.HBM)

SIDE = 4
GROUP = 16
PITCH = 17
BLOCK = 4
CHUNKS = ((0, 16), (16, 32), (48, 16))
SENDS = ((0, 1, 3, 2), (0, 3, 1, 2), (0, 1, 3, 2))
STAGED = 24
HOPS = (0, 1, 3, 2)
LINES = ((0, 2, 1, 3), (0, 3, 1, 2))


def place_of(phase, step):
    place = 0
    for k, other in enumerate(LINES[phase]):
        place = jnp.where(step == other, k, place)
    return place


def hop(k, core):
    return (HOPS[k] * (1 - 2 * core)) % SIDE


def coords(p):
    return p // (2 * SIDE), (p // 2) % SIDE, p % 2


def line_perm(phase, step):
    pairs = []
    for p in range(2 * SIDE * SIDE):
        x, y, core = coords(p)
        if core == phase:
            x = (x + step) % SIDE
        else:
            y = (y + step) % SIDE
        pairs.append((p, (x * SIDE + y) * 2 + core))
    return pairs


def aux_perm(k):
    pairs = 2 * SIDE * SIDE
    return [(a * pairs + p, (a + hop(k, p % 2)) % SIDE * pairs + p) for a in range(SIDE) for p in range(pairs)]


def gather_coeff(coeff_t, integrals):
    own = coeff_t[None]
    tiles = stage_call(integrals)
    line = jnp.concatenate(
        [own] + [lax.ppermute(own, "pair", line_perm(0, step)) for step in LINES[0][1:]], 0
    )
    line, tiles = lax.optimization_barrier((line, tiles))
    mine = [line] + [lax.ppermute(line, "pair", line_perm(1, step)) for step in LINES[1][1:]]
    swap = [(p, p ^ 1) for p in range(2 * SIDE * SIDE)]
    partner = [lax.ppermute(lines, "pair", swap) for lines in mine]
    return mine + partner, tiles


def pick_coeff(nu_ref, count_ref, coeff_refs, cc_ref):
    aux = lax.axis_index("aux")
    pair = lax.axis_index("pair")
    my_x, my_y, my_core = coords(pair)
    width = cc_ref.shape[1] // 3
    for slot in range(3):
        block = nu_ref[0, slot]
        x, y, core = coords(block // 2)
        step_x = (my_x - x + SIDE) % SIDE
        step_y = (my_y - y + SIDE) % SIDE
        first_step = place_of(0, jnp.where(core == 0, step_x, step_y))
        second_step = place_of(1, jnp.where(core == 0, step_y, step_x))
        which = jnp.where(core == my_core, 0, SIDE) + second_step
        lanes = pl.ds(pl.multiple_of((block % 2) * width, width), width)
        live = jnp.broadcast_to(count_ref[...], (16, width)) > slot
        for d in range(SIDE):
            step = jnp.where(my_core == 0, hop(d, 0), hop(d, 1))
            rows = pl.ds(pl.multiple_of(((aux + step) % SIDE) * 16, 16), 16)
            chosen = coeff_refs[0][first_step, rows, lanes]
            for k in range(1, 2 * SIDE):
                chosen = jnp.where(which == k, coeff_refs[k][first_step, rows, lanes], chosen)
            chosen = jnp.where(live, chosen.astype(jnp.float32), 0.0)
            cc_ref[16 * d:16 * d + 16, width * slot:width * (slot + 1)] = chosen.astype(jnp.bfloat16)


def stage_kernel(integrals_ref, tiles_ref, sems):
    copies = []
    for b in range(STAGED // BLOCK):
        copy = pltpu.make_async_copy(integrals_ref.at[:, pl.ds(b * BLOCK, BLOCK)], tiles_ref.at[b], sems.at[b])
        copy.start()
        copies.append(copy)
    for copy in copies:
        copy.wait()


def stage_call(integrals):
    return pl.pallas_call(
        stage_kernel,
        in_specs=[HBM],
        out_specs=VMEM,
        out_shape=jax.ShapeDtypeStruct((STAGED // BLOCK, 3, BLOCK) + integrals.shape[2:], integrals.dtype),
        scratch_shapes=[pltpu.SemaphoreType.DMA((STAGED // BLOCK,))],
        compiler_params=pltpu.CompilerParams(vmem_limit_bytes=40 * 2**20),
        cost_estimate=pl.CostEstimate(
            flops=0, bytes_accessed=2 * STAGED * integrals.shape[2] * 384 * 2, transcendentals=0
        ),
    )(integrals)


def half_body(count, cc_ref, out_refs, acc, block):
    cc = cc_ref[...]
    width = out_refs[0].shape[2]
    parts = width // 128
    for g in range(count // GROUP):
        for k in range(GROUP // BLOCK):
            b = g * (GROUP // BLOCK) + k
            tiles, at = block(b)
            tile = jnp.concatenate([tiles[at, s].reshape(BLOCK * width, 128) for s in range(3)], axis=1)
            prod = lax.dot_general(cc, tile, NT, preferred_element_type=jnp.float32)
            for j in range(BLOCK):
                for q in range(parts):
                    lane = (j * parts + q) * 128
                    acc[g, q, pl.ds(k * BLOCK + j, 64, stride=PITCH), :] = prod[:, lane:lane + 128]
        for d in range(SIDE):
            for q in range(parts):
                for i in range(16):
                    rows = acc[g, q, pl.ds((16 * d + i) * PITCH, GROUP), :].astype(jnp.bfloat16)
                    out_refs[d][i, GROUP * g:GROUP * (g + 1), 128 * q:128 * (q + 1)] = rows


def half_first(count, nu_ref, count_ref, *refs):
    coeff_refs, (tiles, o0, o1, o2, o3, cc_ref, acc) = refs[:2 * SIDE], refs[2 * SIDE:]
    pick_coeff(nu_ref, count_ref, coeff_refs, cc_ref)
    half_body(count, cc_ref, (o0, o1, o2, o3), acc, lambda b: (tiles, b))


def half_next(first, count, held, cc_ref, integrals_ref, *refs):
    o0, o1, o2, o3, acc, tiles, sems = refs[-7:]
    copies = []
    for b in range(held, count // BLOCK):
        copy = pltpu.make_async_copy(
            integrals_ref.at[:, pl.ds(first + b * BLOCK, BLOCK)], tiles.at[b - held], sems.at[b - held]
        )
        copy.start()
        copies.append(copy)

    def block(b):
        if b < held:
            return refs[0], CHUNKS[0][1] // BLOCK + b
        copies[b - held].wait()
        return tiles, b - held

    half_body(count, cc_ref, (o0, o1, o2, o3), acc, block)


def half_call(first, count, integrals, tiles, cc, picked_from):
    width = integrals.shape[2]
    outs = [jax.ShapeDtypeStruct((16, count, width), jnp.bfloat16)] * SIDE
    acc = pltpu.VMEM((count // GROUP, width // 128, 64 * PITCH, 128), jnp.float32)
    cost = pl.CostEstimate(
        flops=2 * count * width * 384 * 256, bytes_accessed=count * width * 384 * 2, transcendentals=0
    )
    if cc is None:
        res = pl.pallas_call(
            functools.partial(half_first, count),
            in_specs=[SMEM] + [VMEM] * (2 * SIDE + 2),
            out_specs=[VMEM] * 5,
            out_shape=outs + [jax.ShapeDtypeStruct((64, 384), jnp.bfloat16)],
            scratch_shapes=[acc],
            compiler_params=pltpu.CompilerParams(vmem_limit_bytes=24 * 2**20),
            cost_estimate=cost,
        )(*picked_from, tiles)
        return res[:SIDE], res[SIDE]
    operands, specs, held = [cc, integrals], [VMEM, HBM], 0
    if first < STAGED:
        operands.append(tiles)
        specs.append(VMEM)
        held = (STAGED - first) // BLOCK
    copied = count // BLOCK - held
    res = pl.pallas_call(
        functools.partial(half_next, first, count, held),
        in_specs=specs,
        out_specs=[VMEM] * 4,
        out_shape=outs,
        scratch_shapes=[
            acc,
            pltpu.VMEM((copied, 3, BLOCK, width, 128), jnp.bfloat16),
            pltpu.SemaphoreType.DMA((copied,)),
        ],
        compiler_params=pltpu.CompilerParams(vmem_limit_bytes=42 * 2**20),
        cost_estimate=cost,
    )(*operands)
    return res, cc


def arrange_kernel(root_ref, after_ref, out_ref, sems):
    aux = lax.axis_index("aux")
    core = lax.axis_index("pair") % 2
    width = out_ref.shape[1] // SIDE
    copies = []
    for k in range(SIDE):
        step = jnp.where(core == 0, hop(k, 0), hop(k, 1))
        source = pl.ds(pl.multiple_of(((aux - step + SIDE) % SIDE) * width, 128), width)
        copy = pltpu.make_async_copy(
            root_ref.at[:, source], out_ref.at[:, pl.ds(k * width, width)], sems.at[k]
        )
        copy.start()
        copies.append(copy)
    for copy in copies:
        copy.wait()


def arrange_root(root, after):
    return pl.pallas_call(
        arrange_kernel,
        in_specs=[HBM, HBM],
        out_specs=VMEM,
        out_shape=jax.ShapeDtypeStruct(root.shape, root.dtype),
        scratch_shapes=[pltpu.SemaphoreType.DMA((SIDE,))],
        compiler_params=pltpu.CompilerParams(vmem_limit_bytes=40 * 2**20),
        cost_estimate=pl.CostEstimate(flops=0, bytes_accessed=root.size // 64, transcendentals=0),
    )(root, after)


def fit_kernel(first, count, order, *refs):
    root_ref, (out_ref, stage, sems) = refs[4], refs[-3:]
    a_refs = [refs[order.index(k)] for k in range(SIDE)]
    rows = 16 * count
    step = stage.shape[3]
    arrived = jnp.concatenate([a[...].reshape(rows, a.shape[2]) for a in a_refs], axis=1)
    copies = []
    for q in range(stage.shape[0]):
        prod = lax.dot_general(
            arrived, root_ref[q * step:(q + 1) * step, :], NT, preferred_element_type=jnp.float32
        )
        stage[q] = prod.astype(jnp.bfloat16).reshape(16, count, step)
        copy = pltpu.make_async_copy(
            stage.at[q], out_ref.at[:, pl.ds(first, count), pl.ds(q * step, step)], sems.at[q]
        )
        copy.start()
        copies.append(copy)
    for copy in copies:
        copy.wait()


def fit_call(first, count, order, arrived, root, out):
    total = root.shape[0]
    step = total if count == GROUP else 512
    operands = [arrived[k] for k in order] + [root]
    specs = [VMEM] * 5
    aliases = {}
    if out is not None:
        operands.append(out)
        specs.append(HBM)
        aliases = {5: 0}
    return pl.pallas_call(
        functools.partial(fit_kernel, first, count, order),
        in_specs=specs,
        out_specs=HBM,
        out_shape=jax.ShapeDtypeStruct((16, 64, total), jnp.bfloat16),
        scratch_shapes=[
            pltpu.VMEM((total // step, 16, count, step), jnp.bfloat16),
            pltpu.SemaphoreType.DMA((total // step,)),
        ],
        input_output_aliases=aliases,
        compiler_params=pltpu.CompilerParams(vmem_limit_bytes=24 * 2**20),
        cost_estimate=pl.CostEstimate(
            flops=32 * count * total * total, bytes_accessed=16 * count * total * 4, transcendentals=0
        ),
    )(*operands)


def shards(integrals, coefficients, nu_blocks, tile_count, metric_root):
    coeff, tiles = gather_coeff(coefficients.T, integrals)
    cc = None
    held = []
    for k, (first, count) in enumerate(CHUNKS):
        if k >= 2:
            cc, held[k - 2] = lax.optimization_barrier((cc, held[k - 2]))
        parts, cc = half_call(first, count, integrals, tiles, cc, [nu_blocks, tile_count] + coeff)
        held.append(
            [parts[0]]
            + [lax.ppermute(parts[d], ("aux", "pair"), aux_perm(d)) for d in range(1, SIDE)]
        )
    root = arrange_root(metric_root, parts[0])
    out = None
    for (first, count), order, arrived in zip(CHUNKS, SENDS, held):
        out = fit_call(first, count, order, arrived, root, out)
    return out.reshape(out.shape[0], out.shape[1], 1, out.shape[2])


def solution(mesh):
    placed = (
        P("pair", None, "aux", None),
        P("pair", None),
        P("aux", "pair"),
        P("aux", "pair"),
        P(),
    )
    return jax.shard_map(
        shards, mesh=mesh, in_specs=placed, out_specs=P("aux", None, "pair", None), check_vma=False
    )
```

```python
import functools

import jax
import jax.numpy as jnp
from jax import lax
from jax.experimental import pallas as pl
from jax.experimental.pallas import tpu as pltpu
from jax.sharding import PartitionSpec as P

NT = (((1,), (1,)), ((), ()))
VMEM = pl.BlockSpec(memory_space=pltpu.VMEM)
SMEM = pl.BlockSpec(memory_space=pltpu.SMEM)
HBM = pl.BlockSpec(memory_space=pltpu.HBM)

SIDE = 4
GROUP = 16
BLOCK = 4
CHUNKS = ((0, 16), (16, 32), (48, 16))
EDGES = {16: (0, 1024, 1536), 32: (0, 512, 1024, 1536)}
SENDS = ((0, 1, 3, 2), (0, 3, 1, 2), (0, 1, 3, 2))
STAGED = 24
HOPS = (0, 1, 3, 2)
LINES = ((0, 2, 1, 3), (0, 3, 1, 2))


def place_of(phase, step):
    place = 0
    for k, other in enumerate(LINES[phase]):
        place = jnp.where(step == other, k, place)
    return place


def hop(k, core):
    return (HOPS[k] * (1 - 2 * core)) % SIDE


def coords(p):
    return p // (2 * SIDE), (p // 2) % SIDE, p % 2


def line_perm(phase, step):
    pairs = []
    for p in range(2 * SIDE * SIDE):
        x, y, core = coords(p)
        if core == phase:
            x = (x + step) % SIDE
        else:
            y = (y + step) % SIDE
        pairs.append((p, (x * SIDE + y) * 2 + core))
    return pairs


def aux_perm(k):
    pairs = 2 * SIDE * SIDE
    return [(a * pairs + p, (a + hop(k, p % 2)) % SIDE * pairs + p) for a in range(SIDE) for p in range(pairs)]


def gather_coeff(coeff_t, integrals):
    own = coeff_t[None]
    tiles = stage_call(integrals)
    line = jnp.concatenate(
        [own] + [lax.ppermute(own, "pair", line_perm(0, step)) for step in LINES[0][1:]], 0
    )
    line, tiles = lax.optimization_barrier((line, tiles))
    mine = [line] + [lax.ppermute(line, "pair", line_perm(1, step)) for step in LINES[1][1:]]
    swap = [(p, p ^ 1) for p in range(2 * SIDE * SIDE)]
    partner = [lax.ppermute(lines, "pair", swap) for lines in mine]
    return mine + partner, tiles


def pick_coeff(nu_ref, count_ref, coeff_refs, cc_ref):
    aux = lax.axis_index("aux")
    pair = lax.axis_index("pair")
    my_x, my_y, my_core = coords(pair)
    width = cc_ref.shape[1] // 3
    for slot in range(3):
        block = nu_ref[0, slot]
        x, y, core = coords(block // 2)
        step_x = (my_x - x + SIDE) % SIDE
        step_y = (my_y - y + SIDE) % SIDE
        first_step = place_of(0, jnp.where(core == 0, step_x, step_y))
        second_step = place_of(1, jnp.where(core == 0, step_y, step_x))
        which = jnp.where(core == my_core, 0, SIDE) + second_step
        lanes = pl.ds(pl.multiple_of((block % 2) * width, width), width)
        live = jnp.broadcast_to(count_ref[...], (16, width)) > slot
        for d in range(SIDE):
            step = jnp.where(my_core == 0, hop(d, 0), hop(d, 1))
            rows = pl.ds(pl.multiple_of(((aux + step) % SIDE) * 16, 16), 16)
            chosen = coeff_refs[0][first_step, rows, lanes]
            for k in range(1, 2 * SIDE):
                chosen = jnp.where(which == k, coeff_refs[k][first_step, rows, lanes], chosen)
            chosen = jnp.where(live, chosen.astype(jnp.float32), 0.0)
            cc_ref[16 * d:16 * d + 16, width * slot:width * (slot + 1)] = chosen.astype(jnp.bfloat16)


def stage_kernel(integrals_ref, tiles_ref, sems):
    copies = []
    for b in range(STAGED // BLOCK):
        copy = pltpu.make_async_copy(integrals_ref.at[:, pl.ds(b * BLOCK, BLOCK)], tiles_ref.at[b], sems.at[b])
        copy.start()
        copies.append(copy)
    for copy in copies:
        copy.wait()


def stage_call(integrals):
    return pl.pallas_call(
        stage_kernel,
        in_specs=[HBM],
        out_specs=VMEM,
        out_shape=jax.ShapeDtypeStruct((STAGED // BLOCK, 3, BLOCK) + integrals.shape[2:], integrals.dtype),
        scratch_shapes=[pltpu.SemaphoreType.DMA((STAGED // BLOCK,))],
        compiler_params=pltpu.CompilerParams(vmem_limit_bytes=40 * 2**20),
        cost_estimate=pl.CostEstimate(
            flops=0, bytes_accessed=2 * STAGED * integrals.shape[2] * 384 * 2, transcendentals=0
        ),
    )(integrals)


def half_body(count, cc_ref, out_refs, acc, block):
    cc = cc_ref[...]
    width = out_refs[0].shape[2]
    parts = width // 128
    for g in range(count // GROUP):
        for k in range(GROUP // BLOCK):
            b = g * (GROUP // BLOCK) + k
            tiles, at = block(b)
            tile = jnp.concatenate([tiles[at, s].reshape(BLOCK * width, 128) for s in range(3)], axis=1)
            prod = lax.dot_general(cc, tile, NT, preferred_element_type=jnp.float32)
            for j in range(BLOCK):
                for q in range(parts):
                    lane = (j * parts + q) * 128
                    acc[g, q, pl.ds(k * BLOCK + j, 64, stride=GROUP), :] = prod[:, lane:lane + 128]
        for d in range(SIDE):
            for q in range(parts):
                rows = acc[g, q, 256 * d:256 * d + 256, :].astype(jnp.bfloat16)
                out_refs[d][:, GROUP * g:GROUP * (g + 1), 128 * q:128 * (q + 1)] = rows.reshape(16, GROUP, 128)


def half_first(count, nu_ref, count_ref, *refs):
    coeff_refs, (tiles, o0, o1, o2, o3, cc_ref, acc) = refs[:2 * SIDE], refs[2 * SIDE:]
    pick_coeff(nu_ref, count_ref, coeff_refs, cc_ref)
    half_body(count, cc_ref, (o0, o1, o2, o3), acc, lambda b: (tiles, b))


def half_next(first, count, held, cc_ref, integrals_ref, *refs):
    o0, o1, o2, o3, acc, tiles, sems = refs[-7:]
    copies = []
    for b in range(held, count // BLOCK):
        copy = pltpu.make_async_copy(
            integrals_ref.at[:, pl.ds(first + b * BLOCK, BLOCK)], tiles.at[b - held], sems.at[b - held]
        )
        copy.start()
        copies.append(copy)

    def block(b):
        if b < held:
            return refs[0], CHUNKS[0][1] // BLOCK + b
        copies[b - held].wait()
        return tiles, b - held

    half_body(count, cc_ref, (o0, o1, o2, o3), acc, block)


def half_call(first, count, integrals, tiles, cc, picked_from):
    width = integrals.shape[2]
    outs = [jax.ShapeDtypeStruct((16, count, width), jnp.bfloat16)] * SIDE
    acc = pltpu.VMEM((count // GROUP, width // 128, 64 * GROUP, 128), jnp.float32)
    cost = pl.CostEstimate(
        flops=2 * count * width * 384 * 256, bytes_accessed=count * width * 384 * 2, transcendentals=0
    )
    if cc is None:
        res = pl.pallas_call(
            functools.partial(half_first, count),
            in_specs=[SMEM] + [VMEM] * (2 * SIDE + 2),
            out_specs=[VMEM] * 5,
            out_shape=outs + [jax.ShapeDtypeStruct((64, 384), jnp.bfloat16)],
            scratch_shapes=[acc],
            compiler_params=pltpu.CompilerParams(vmem_limit_bytes=24 * 2**20),
            cost_estimate=cost,
        )(*picked_from, tiles)
        return res[:SIDE], res[SIDE]
    operands, specs, held = [cc, integrals], [VMEM, HBM], 0
    if first < STAGED:
        operands.append(tiles)
        specs.append(VMEM)
        held = (STAGED - first) // BLOCK
    copied = count // BLOCK - held
    res = pl.pallas_call(
        functools.partial(half_next, first, count, held),
        in_specs=specs,
        out_specs=[VMEM] * 4,
        out_shape=outs,
        scratch_shapes=[
            acc,
            pltpu.VMEM((copied, 3, BLOCK, width, 128), jnp.bfloat16),
            pltpu.SemaphoreType.DMA((copied,)),
        ],
        compiler_params=pltpu.CompilerParams(vmem_limit_bytes=42 * 2**20),
        cost_estimate=cost,
    )(*operands)
    return res, cc


def arrange_kernel(root_ref, after_ref, out_ref, sems):
    aux = lax.axis_index("aux")
    core = lax.axis_index("pair") % 2
    width = out_ref.shape[1] // SIDE
    copies = []
    for k in range(SIDE):
        step = jnp.where(core == 0, hop(k, 0), hop(k, 1))
        source = pl.ds(pl.multiple_of(((aux - step + SIDE) % SIDE) * width, 128), width)
        copy = pltpu.make_async_copy(
            root_ref.at[:, source], out_ref.at[:, pl.ds(k * width, width)], sems.at[k]
        )
        copy.start()
        copies.append(copy)
    for copy in copies:
        copy.wait()


def arrange_root(root, after):
    return pl.pallas_call(
        arrange_kernel,
        in_specs=[HBM, HBM],
        out_specs=VMEM,
        out_shape=jax.ShapeDtypeStruct(root.shape, root.dtype),
        scratch_shapes=[pltpu.SemaphoreType.DMA((SIDE,))],
        compiler_params=pltpu.CompilerParams(vmem_limit_bytes=40 * 2**20),
        cost_estimate=pl.CostEstimate(flops=0, bytes_accessed=root.size // 64, transcendentals=0),
    )(root, after)


def fit_kernel(first, count, order, *refs):
    root_ref, (out_ref, stage, sems) = refs[4], refs[-3:]
    a_refs = [refs[order.index(k)] for k in range(SIDE)]
    rows = 16 * count
    arrived = jnp.concatenate([a[...].reshape(rows, a.shape[2]) for a in a_refs], axis=1)
    copies = []
    for q, (begin, end) in enumerate(zip(EDGES[count], EDGES[count][1:])):
        prod = lax.dot_general(arrived, root_ref[begin:end, :], NT, preferred_element_type=jnp.float32)
        stage[:, :, begin:end] = prod.astype(jnp.bfloat16).reshape(16, count, end - begin)
        copy = pltpu.make_async_copy(
            stage.at[:, :, pl.ds(begin, end - begin)],
            out_ref.at[:, pl.ds(first, count), pl.ds(begin, end - begin)],
            sems.at[q],
        )
        copy.start()
        copies.append(copy)
    for copy in copies:
        copy.wait()


def fit_call(first, count, order, arrived, root, out):
    total = root.shape[0]
    operands = [arrived[k] for k in order] + [root]
    specs = [VMEM] * 5
    aliases = {}
    if out is not None:
        operands.append(out)
        specs.append(HBM)
        aliases = {5: 0}
    return pl.pallas_call(
        functools.partial(fit_kernel, first, count, order),
        in_specs=specs,
        out_specs=HBM,
        out_shape=jax.ShapeDtypeStruct((16, 64, total), jnp.bfloat16),
        scratch_shapes=[
            pltpu.VMEM((16, count, total), jnp.bfloat16),
            pltpu.SemaphoreType.DMA((len(EDGES[count]) - 1,)),
        ],
        input_output_aliases=aliases,
        compiler_params=pltpu.CompilerParams(vmem_limit_bytes=24 * 2**20),
        cost_estimate=pl.CostEstimate(
            flops=32 * count * total * total, bytes_accessed=16 * count * total * 4, transcendentals=0
        ),
    )(*operands)


def shards(integrals, coefficients, nu_blocks, tile_count, metric_root):
    coeff, tiles = gather_coeff(coefficients.T, integrals)
    cc = None
    held = []
    for k, (first, count) in enumerate(CHUNKS):
        if k >= 2:
            cc, held[k - 2] = lax.optimization_barrier((cc, held[k - 2]))
        parts, cc = half_call(first, count, integrals, tiles, cc, [nu_blocks, tile_count] + coeff)
        held.append(
            [parts[0]]
            + [lax.ppermute(parts[d], ("aux", "pair"), aux_perm(d)) for d in range(1, SIDE)]
        )
    root = arrange_root(metric_root, parts[0])
    out = None
    for (first, count), order, arrived in zip(CHUNKS, SENDS, held):
        out = fit_call(first, count, order, arrived, root, out)
    return out.reshape(out.shape[0], out.shape[1], 1, out.shape[2])


def solution(mesh):
    placed = (
        P("pair", None, "aux", None),
        P("pair", None),
        P("aux", "pair"),
        P("aux", "pair"),
        P(),
    )
    return jax.shard_map(
        shards, mesh=mesh, in_specs=placed, out_specs=P("aux", None, "pair", None), check_vma=False
    )
```
